32 devices in a mesh: subj: 8 (over z, y), slab: 4 (over x, core).
Axes of the slice: x: 2, y: 2, z: 4, core: 2. Of those that a mesh axis runs over, the one named last changes fastest.
Arguments:
- data_rhs: float32 [8, 16, 16, 1536], P('subj', None, 'slab'), may hold values from -12 to 12
- inv_var: float32 [8, 16, 1536], P('subj', 'slab'), may hold values from 0.01 to 0.3
- design: float32 [8, 16], P('subj'), may hold values from 0.5 to 4
- keep_mask: int32 [8, 16, 1536], P('subj', 'slab'), may hold values 0 or 1
- brain_mask: int32 [16, 1536], P('slab'), may hold values 0 or 1
- tissue: int32 [16, 1536], P('slab'), may hold values from 0 to 2
- kappa_sq: float32 [3, 16], replicated, may hold values from 0.005 to 0.5
- prior_scale: float32 [16], replicated, may hold values from 0.5 to 2
- mean_field: float32 [16, 16, 1536], P(None, 'slab', 'subj'), may hold values from -6 to 6
- pop_noise: float32 [16, 16, 1536], P(None, 'slab', 'subj'), may hold values from -6 to 6
Outputs:
- subject_fields: float32 [8, 16, 16, 1536], P('subj', None, 'slab')
- new_mean: float32 [16, 16, 1536], P(None, 'slab', 'subj')
The draws below stay inside these ranges and needn't reach their ends.
All inputs are finite; a program needn't handle non-finite values. No bound on the sum of `keep_mask` or of `brain_mask` on one device may be relied on, other than what follows from the above.
Results may differ from the reference program's by a relative error of at most 0.00016.
Values sent between devices are 32-bit elements; how exact they have to be, the bound alone decides.
No kernel may reach another device: no remote copies, remote signals or barrier semaphores. Data moves between devices by JAX's collectives and lax.ppermute only.
A program may use at most 64 MiB of HBM per device.

```python
import math
import jax
import jax.numpy as jnp
from jax import lax

K = 16
CLASSES = 3
ITERS = 8
CX = 64
CY = 24
SUBJECTS = 8
NZ = 16


def touch_ends(values, stream_key, least, top_value):
    dims = values.shape
    index_at = [jax.random.randint(jax.random.fold_in(stream_key, axis), (), 0, dims[axis]) for axis in range(len(dims))]
    values = values.at[tuple(index_at)].set(least)
    longest = dims.index(max(dims))
    index_at[longest] = (index_at[longest] + 1) % dims[longest]
    return values.at[tuple(index_at)].set(top_value)


def with_spikes(result, rng, source, target, shards_of, factor):
    def block_of(dim):
        return (jnp.arange(result.shape[dim]) // (result.shape[dim] // shards_of)).reshape((-1,) + (1,) * (result.ndim - 1 - dim))

    near = jax.random.permutation(rng, shards_of)[block_of(target)]
    far = (block_of(target) + shards_of // 2) % shards_of
    return jnp.where((block_of(source) == near) | (block_of(source) == far), factor * result, result)


def block_levels(own_key, shape, split, low, top_value):
    factor_of = 1.0
    for dim, parts in split:
        heights = jax.random.uniform(jax.random.fold_in(jax.random.fold_in(own_key, 6), dim), (parts,), jnp.float32, low / len(split), top_value / len(split))
        factor_of = factor_of * jnp.repeat(jnp.exp(heights), shape[dim] // parts).reshape((-1,) + (1,) * (len(shape) - 1 - dim))
    return factor_of


def bell_draw(own_key, extent, width, reach, cuts=(), dtype=jnp.bfloat16):
    result = width * jax.random.normal(own_key, extent, jnp.float32)
    if cuts:
        result = result * block_levels(own_key, extent, cuts, -0.22, 0.18)
    return jnp.clip(result, -reach, reach).astype(dtype)


def heavy_noise(rng, dims, deviation, bound, pieces, heavy, held_as=jnp.bfloat16):
    values = deviation * jax.random.normal(rng, dims, jnp.float32)
    if pieces:
        values = values * block_levels(rng, dims, pieces, -0.22, 0.18)
    return jnp.clip(with_spikes(values, jax.random.fold_in(rng, 3), *heavy), -bound, bound).astype(held_as)


def setup_inputs(seed: int = 0) -> dict:
    keys = jax.random.split(jax.random.key(seed), 11)
    data_rhs = heavy_noise(keys[0], (SUBJECTS, K, NZ, CY * CX), 2.0, 12.0, ((0, 8), (2, 4)), (0, 3, 8, 2.0), jnp.float32)
    inv_var = jnp.clip(jnp.exp(math.log(0.3) - 3.4011974 * jax.random.uniform(keys[1], (SUBJECTS, NZ, CY * CX), jnp.float32) ** block_levels(keys[1], (SUBJECTS, NZ, CY * CX), ((0, 8), (1, 4)), -0.2, 0.2)), 0.01, 0.3)
    design = jnp.clip(jnp.exp(math.log(4.0) - 2.0794415 * jax.random.uniform(keys[2], (SUBJECTS, K), jnp.float32) ** block_levels(keys[2], (SUBJECTS, K), ((0, 8),), -0.2, 0.2)), 0.5, 4.0)
    keep_mask = touch_ends((jax.random.randint(keys[3], (SUBJECTS, NZ, CY * CX), 0, 10) < 9).astype(jnp.int32), jax.random.fold_in(keys[3], 1), 0, 1)
    brain_mask = touch_ends((jax.random.randint(keys[4], (NZ, CY * CX), 0, 5) < 4).astype(jnp.int32), jax.random.fold_in(keys[4], 1), 0, 1)
    tissue = touch_ends(jax.random.randint(keys[5], (NZ, CY * CX), 0, CLASSES), jax.random.fold_in(keys[5], 1), 0, CLASSES - 1).astype(jnp.int32)
    kappa_sq = jnp.clip(jnp.exp(jax.random.uniform(keys[6], (CLASSES, K), jnp.float32, math.log(0.005), math.log(0.5))), 0.005, 0.5)
    prior_scale = jnp.clip(jnp.exp(jax.random.uniform(keys[7], (K,), jnp.float32, math.log(0.5), math.log(2.0))), 0.5, 2.0)
    mean_field = bell_draw(keys[8], (K, NZ, CY * CX), 1.0, 6.0, ((1, 4), (2, 8)), jnp.float32)
    pop_noise = bell_draw(keys[9], (K, NZ, CY * CX), 1.0, 6.0, ((1, 4), (2, 8)), jnp.float32)
    return dict(data_rhs=data_rhs, inv_var=inv_var, design=design, keep_mask=keep_mask, brain_mask=brain_mask, tissue=tissue, kappa_sq=kappa_sq, prior_scale=prior_scale, mean_field=mean_field, pop_noise=pop_noise)


MEAN_PRECISION = 1.0

def prior_apply(values, kappa_field, prior_scale):
    regressors = values.shape[0]
    volume = values.reshape(regressors, NZ, CY, CX)
    padded = jnp.pad(volume, ((0, 0), (1, 1), (1, 1), (1, 1)))
    beside = padded[:, 2:, 1:-1, 1:-1] + padded[:, :-2, 1:-1, 1:-1]
    beside = beside + padded[:, 1:-1, 2:, 1:-1] + padded[:, 1:-1, :-2, 1:-1]
    beside = beside + padded[:, 1:-1, 1:-1, 2:] + padded[:, 1:-1, 1:-1, :-2]
    beside = beside.reshape(values.shape)
    return prior_scale[:, None, None] * ((6.0 + kappa_field) * values - beside)

def reference(data_rhs, inv_var, design, keep_mask, brain_mask, tissue, kappa_sq, prior_scale, mean_field, pop_noise):
    kappa_field = jnp.transpose(kappa_sq[tissue], (2, 0, 1))
    in_brain = brain_mask.astype(jnp.float32)
    prior_mean = prior_apply(mean_field, kappa_field, prior_scale)

    def solve_one(inputs):
        data_term, variance_inv, design_row, keep_row = inputs
        data_prec = design_row[:, None, None] * (variance_inv * in_brain * keep_row.astype(jnp.float32))[None]

        def operate(values):
            return data_prec * values + prior_apply(values, kappa_field, prior_scale)
        right_side = data_term + prior_mean
        solution = jnp.zeros_like(right_side)
        residual = right_side
        direction = right_side
        norm_now = lax.optimization_barrier(jnp.sum(residual * residual, axis=(1, 2)))
        for iteration in range(ITERS):
            applied = operate(direction)
            step_size = norm_now / lax.optimization_barrier(jnp.sum(direction * applied, axis=(1, 2)))
            solution = solution + step_size[:, None, None] * direction
            if iteration + 1 < ITERS:
                residual = residual - step_size[:, None, None] * applied
                norm_next = lax.optimization_barrier(jnp.sum(residual * residual, axis=(1, 2)))
                direction = residual + (norm_next / norm_now)[:, None, None] * direction
                norm_now = norm_next
        return solution
    fields_out = lax.map(solve_one, (data_rhs, inv_var, design, keep_mask))
    divisor = SUBJECTS + MEAN_PRECISION
    new_mean = lax.optimization_barrier(jnp.sum(fields_out, axis=0)) / divisor + pop_noise / math.sqrt(divisor)
    return (fields_out, new_mean)
```

```python
import math

import jax
import jax.numpy as jnp
from jax import lax
from jax.experimental import pallas as pl
from jax.experimental.pallas import tpu as pltpu
from jax.sharding import PartitionSpec as P

CLASSES = 3
ITERS = 8
CX = 64
LANES = 128
ROWS = 8


MEAN_PRECISION = 1.0


def beside_of(tiles):
    shape = tiles[0][0].shape
    lane = lax.broadcasted_iota(jnp.int32, shape, 1)
    row = lax.broadcasted_iota(jnp.int32, shape, 0)
    low = lane < CX
    first, last = lane % CX == 0, lane % CX == CX - 1
    planes, groups = len(tiles), len(tiles[0])
    turned = [[pltpu.roll(v, CX, 1) for v in line] for line in tiles]
    down = [[pltpu.roll(v, 1, 0) for v in line] for line in tiles]
    up = [[pltpu.roll(v, ROWS - 1, 0) for v in line] for line in tiles]
    zero = jnp.zeros(shape, jnp.float32)
    out = []
    for t in range(planes):
        line = []
        for g in range(groups):
            v = tiles[t][g]
            total = jnp.where(first, 0.0, pltpu.roll(v, 1, 1)) + jnp.where(last, 0.0, pltpu.roll(v, LANES - 1, 1))
            before = turned[t][g - 1] if g else zero
            after = turned[t][g + 1] if g + 1 < groups else zero
            total = total + (turned[t][g] + jnp.where(low, before, after))
            below = down[t - 1][g] if t else zero
            above = up[t + 1][g] if t + 1 < planes else zero
            total = total + (jnp.where(row == 0, below, down[t][g]) + jnp.where(row == ROWS - 1, above, up[t][g]))
            line.append(total)
        out.append(line)
    return out


def cg_kernel(design, kappa, scale, rhs, mean, factor, tissue, out, diag, direction, residual, applied):
    regressors, depth, cells = rhs.shape
    planes, groups = depth // ROWS, cells // LANES
    everywhere = [(t, g) for t in range(planes) for g in range(groups)]

    def at(t, g):
        return pl.ds(t * ROWS, ROWS), pl.ds(g * LANES, LANES)

    def load(ref, r):
        return [[ref[(r,) + at(t, g)] for g in range(groups)] for t in range(planes)]

    def whole_sum(parts):
        while len(parts) > 1:
            parts = [sum(parts[i : i + 2][1:], parts[i]) for i in range(0, len(parts), 2)]
        return jnp.sum(parts[0], axis=(0, 1), keepdims=True)

    norms = []
    for r in range(regressors):
        beside = beside_of(load(mean, r))
        squares = []
        for t, g in everywhere:
            where = at(t, g)
            label = tissue[where]
            shifted = jnp.full(label.shape, 6.0, jnp.float32)
            for c in range(CLASSES):
                shifted = shifted + jnp.where(label == c, kappa[c, r], 0.0)
            diag[(r,) + where] = (design[r] / scale[r]) * factor[where] + shifted
            right = rhs[(r,) + where] + scale[r] * (shifted * mean[(r,) + where] - beside[t][g])
            residual[(r,) + where] = right
            direction[(r,) + where] = right
            out[(r,) + where] = jnp.zeros_like(right)
            squares.append(right * right)
        norms.append(whole_sum(squares))

    def step(norms, last):
        steps = []
        for r in range(regressors):
            tiles = load(direction, r)
            beside = beside_of(tiles)
            products = []
            for t, g in everywhere:
                value = diag[(r,) + at(t, g)] * tiles[t][g] - beside[t][g]
                if not last:
                    applied[(r,) + at(t, g)] = value
                products.append(tiles[t][g] * value)
            steps.append(norms[r] / whole_sum(products))
        after = []
        for r in range(regressors):
            squares = []
            for t, g in everywhere:
                where = (r,) + at(t, g)
                value = out[where] + steps[r] * direction[where]
                if last:
                    out[where] = value / scale[r]
                else:
                    out[where] = value
                    left = residual[where] - steps[r] * applied[where]
                    residual[where] = left
                    squares.append(left * left)
            if not last:
                after.append(whole_sum(squares))
        if last:
            return
        for r in range(regressors):
            ratio = after[r] / norms[r]
            for t, g in everywhere:
                where = (r,) + at(t, g)
                direction[where] = residual[where] + ratio * direction[where]
        return tuple(after)

    norms = lax.fori_loop(0, ITERS - 1, lambda _, n: step(n, False), tuple(norms))
    step(norms, True)


def conjugate_gradients(design, kappa, scale, rhs, mean, factor, tissue):
    smem = pl.BlockSpec(memory_space=pltpu.SMEM)
    vmem = pl.BlockSpec(memory_space=pltpu.VMEM)
    field = pltpu.VMEM(rhs.shape, jnp.float32)
    return pl.pallas_call(
        cg_kernel,
        out_shape=jax.ShapeDtypeStruct(rhs.shape, jnp.float32),
        in_specs=[smem] * 3 + [vmem] * 4,
        out_specs=vmem,
        scratch_shapes=[field] * 4,
        compiler_params=pltpu.CompilerParams(vmem_limit_bytes=32 * 2**20),
    )(design, kappa, scale, rhs, mean, factor, tissue)


def exchange(blocks, axis):
    count = lax.axis_size(axis)
    me = lax.axis_index(axis)
    out = blocks
    for k in range(1, count):
        peer = me ^ k
        sent = lax.dynamic_index_in_dim(blocks, peer, 0, keepdims=False)
        got = lax.ppermute(sent, axis, [(i, i ^ k) for i in range(count)])
        out = lax.dynamic_update_index_in_dim(out, got, peer, 0)
    return out


def local(
    data_rhs,
    inv_var,
    design,
    keep_mask,
    brain_mask,
    tissue,
    kappa_sq,
    prior_scale,
    mean_field,
    pop_noise,
):
    subjects, slabs = lax.axis_size("subj"), lax.axis_size("slab")
    mine = lax.axis_index("slab")
    total, depth, cells = data_rhs.shape[1:]
    share = mean_field.shape[2]
    part = total // slabs

    factor = inv_var * brain_mask.astype(jnp.float32) * keep_mask.astype(jnp.float32)
    planes = jnp.concatenate([factor, tissue.astype(jnp.float32)[None]])
    blocks = jnp.concatenate(
        [
            data_rhs.reshape(slabs, part, depth, cells),
            jnp.broadcast_to(planes[None], (slabs,) + planes.shape),
        ],
        axis=1,
    )
    blocks = exchange(blocks, "slab")
    blocks = jnp.transpose(blocks, (1, 0, 2, 3)).reshape(part + 2, slabs * depth, cells)

    means = jnp.broadcast_to(mean_field.reshape(1, slabs, part, depth, share), (subjects, slabs, part, depth, share))
    means = means.reshape(subjects * slabs, part, depth, share)
    means = lax.all_to_all(means, ("subj", "slab"), 0, 0, tiled=True)
    means = means.reshape(subjects, slabs, part, depth, share)
    means = jnp.transpose(means, (2, 1, 3, 0, 4)).reshape(part, slabs * depth, cells)

    fields = conjugate_gradients(
        lax.dynamic_slice_in_dim(design[0], mine * part, part),
        lax.dynamic_slice_in_dim(kappa_sq, mine * part, part, axis=1),
        lax.dynamic_slice_in_dim(prior_scale, mine * part, part),
        blocks[:part],
        means,
        blocks[part],
        blocks[part + 1].astype(jnp.int32),
    )

    by_slab = fields.reshape(part, slabs, depth, cells)
    solution = exchange(jnp.transpose(by_slab, (1, 0, 2, 3)), "slab").reshape(1, total, depth, cells)
    pieces = jnp.transpose(by_slab.reshape(part, slabs, depth, subjects, share), (3, 1, 0, 2, 4))
    pieces = lax.all_to_all(pieces.reshape(subjects * slabs, part, depth, share), ("subj", "slab"), 0, 0, tiled=True)
    summed = jnp.sum(pieces.reshape(subjects, total, depth, share), axis=0)
    divisor = subjects + MEAN_PRECISION
    new_mean = summed / divisor + pop_noise / math.sqrt(divisor)
    return (solution, new_mean)


def solution(mesh):
    in_specs = (
        P("subj", None, "slab", None),
        P("subj", "slab", None),
        P("subj", None),
        P("subj", "slab", None),
        P("slab", None),
        P("slab", None),
        P(),
        P(),
        P(None, "slab", "subj"),
        P(None, "slab", "subj"),
    )
    out_specs = (P("subj", None, "slab", None), P(None, "slab", "subj"))
    return jax.shard_map(local, mesh=mesh, in_specs=in_specs, out_specs=out_specs, check_vma=False)
```

```python
import functools
import math

import jax
import jax.numpy as jnp
from jax import lax
from jax.experimental import pallas as pl
from jax.experimental.pallas import tpu as pltpu
from jax.sharding import PartitionSpec as P

CLASSES = 3
ITERS = 8
CX = 64
LANES = 128
ROWS = 8
DEPTH = 4


MEAN_PRECISION = 1.0


def stencil_matrix(pieces):
    come = lax.broadcasted_iota(jnp.int32, (pieces * LANES, LANES), 0) % LANES
    go = lax.broadcasted_iota(jnp.int32, (pieces * LANES, LANES), 1)
    row = ((come < CX) == (go < CX)) & (abs(come - go) == 1)
    return jnp.where(row | (abs(come - go) == CX), 1.0, 0.0).astype(jnp.bfloat16)


def beside_of(tiles):
    shape = tiles[0][0].shape
    row = lax.broadcasted_iota(jnp.int32, shape, 0)
    low = low_lanes(shape)
    planes, groups = len(tiles), len(tiles[0])
    zero = jnp.zeros(shape, jnp.float32)
    whole = jnp.concatenate([tiles[t][g] for g in range(groups) for t in range(planes)], axis=0)
    coarse = whole.astype(jnp.bfloat16)
    fine = (whole - coarse.astype(jnp.float32)).astype(jnp.bfloat16)
    inside = jnp.dot(
        jnp.concatenate([coarse, fine], axis=1), stencil_matrix(2), preferred_element_type=jnp.float32
    )
    down = [[pltpu.roll(v, 1, 0) for v in line] for line in tiles]
    up = [[pltpu.roll(v, ROWS - 1, 0) for v in line] for line in tiles]
    out = []
    for t in range(planes):
        line = []
        for g in range(groups):
            start = (g * planes + t) * ROWS
            before = tiles[t][g - 1] if g else zero
            after = tiles[t][g + 1] if g + 1 < groups else zero
            total = inside[start : start + ROWS] + pltpu.roll(jnp.where(low, after, before), CX, 1)
            below = down[t - 1][g] if t else zero
            above = up[t + 1][g] if t + 1 < planes else zero
            total = total + (jnp.where(row == 0, below, down[t][g]) + jnp.where(row == ROWS - 1, above, up[t][g]))
            line.append(total)
        out.append(line)
    return out


def mixed(one, two):
    half = lax.broadcasted_iota(jnp.int32, one.shape, 0) < DEPTH
    return jnp.where(half, one, pltpu.roll(two, DEPTH, 0)), jnp.where(half, pltpu.roll(one, DEPTH, 0), two)


def low_lanes(shape):
    return lax.broadcasted_iota(jnp.int32, shape, 1) < CX


def fits_packing(part, depth, share, slabs, subjects):
    return part == 4 and depth == DEPTH and 2 * share == 3 * LANES and slabs % 2 == 0 and subjects % 2 == 0


def pack_kernel(mean, out):
    odd = lax.axis_index("subj") % 2 == 1
    slabs = mean.shape[0] // 4
    for j in range(slabs):
        wide, narrow = [], []
        for k in (4 * j, 4 * j + 2):
            wide.append(jnp.concatenate([mean[k, :, :LANES], mean[k + 1, :, :LANES]], axis=0))
            rest = jnp.concatenate([mean[k, :, LANES:], mean[k + 1, :, LANES:]], axis=0)
            narrow.append(jnp.concatenate([rest, rest], axis=1))
        low = low_lanes(wide[0].shape)
        turned = [pltpu.roll(w, CX, 1) for w in wide]
        rows = [jnp.where(odd, jnp.where(low, turned[i], narrow[i]), wide[i]) for i in (0, 1)]
        rows.append(jnp.where(odd, jnp.where(low, wide[1], turned[0]), jnp.where(low, narrow[0], narrow[1])))
        for s in range(out.shape[0] // slabs):
            for i in range(3):
                out[s * slabs + j, ROWS * i : ROWS * (i + 1)] = rows[i]


def pack(mean, subjects, slabs):
    return pl.pallas_call(
        pack_kernel,
        out_shape=jax.ShapeDtypeStruct((subjects * slabs, 3 * ROWS, LANES), jnp.float32),
        in_specs=[pl.BlockSpec(memory_space=pltpu.VMEM)],
        out_specs=pl.BlockSpec(memory_space=pltpu.VMEM),
    )(mean)


def finish_kernel(pieces, noise, out, *, slabs, subjects):
    odd = lax.axis_index("subj") % 2 == 1
    divisor = subjects + MEAN_PRECISION
    for j in range(slabs):
        rows = []
        for i in range(3):
            total = pieces[j, ROWS * i : ROWS * (i + 1)]
            for s in range(1, subjects):
                total = total + pieces[s * slabs + j, ROWS * i : ROWS * (i + 1)]
            rows.append(total / divisor)
        low = low_lanes(rows[0].shape)
        turned = [pltpu.roll(v, CX, 1) for v in rows]
        for i in (0, 1):
            mid = (rows[2], turned[2])
            wide = jnp.where(odd, jnp.where(low, mid[1 - i], turned[i]), rows[i])
            narrow = jnp.where(odd, turned[i], mid[i])
            for n in (0, 1):
                k, here = 4 * j + 2 * i + n, slice(DEPTH * n, DEPTH * (n + 1))
                out[k, :, :LANES] = wide[here] + noise[k, :, :LANES] / math.sqrt(divisor)
                out[k, :, LANES:] = narrow[here, :CX] + noise[k, :, LANES:] / math.sqrt(divisor)


def finish(pieces, noise, subjects, slabs):
    return pl.pallas_call(
        functools.partial(finish_kernel, slabs=slabs, subjects=subjects),
        out_shape=jax.ShapeDtypeStruct(noise.shape, jnp.float32),
        in_specs=[pl.BlockSpec(memory_space=pltpu.VMEM)] * 2,
        out_specs=pl.BlockSpec(memory_space=pltpu.VMEM),
    )(pieces, noise)


def cg_kernel(design, kappa, scale, rhs, mean, factor, tissue, out, *refs, packed, slabs):
    pieces = refs[0] if packed else None
    diag, direction, residual, applied, mean_scratch = refs[-5:]
    regressors, depth, cells = rhs.shape
    planes, groups = depth // ROWS, cells // LANES
    everywhere = [(t, g) for t in range(planes) for g in range(groups)]
    low = low_lanes((ROWS, LANES))

    def at(t, g):
        return pl.ds(t * ROWS, ROWS), pl.ds(g * LANES, LANES)

    def tiles_of(ref, r):
        return [[ref[(r,) + at(t, g)] for g in range(groups)] for t in range(planes)]

    def add_up(parts):
        while len(parts) > 1:
            parts = [sum(parts[i : i + 2][1:], parts[i]) for i in range(0, len(parts), 2)]
        return parts[0]

    def reduced(parts):
        own, across, twice = (jnp.sum(p, axis=(0, 1), keepdims=True) for p in parts)
        size = own / across
        return size, size * (twice / across) - 1.0

    def unpack():
        for t, g in everywhere:
            pair, m = g // 3, g % 3
            even, odd = 2 * pair * slabs + 2 * t, (2 * pair + 1) * slabs + 2 * t
            for i in (0, 1):
                two = []
                for j in (0, 1):
                    if m == 1:
                        first, second = mean[even + j, 2 * ROWS :], mean[odd + j, 2 * ROWS :]
                        if i == 0:
                            two.append(jnp.where(low, first, second))
                        else:
                            two.append(pltpu.roll(jnp.where(low, second, first), CX, 1))
                    else:
                        two.append(mean[(even if m == 0 else odd) + j, ROWS * i : ROWS * (i + 1)])
                for n, value in enumerate(mixed(*two)):
                    mean_scratch[(2 * i + n,) + at(t, g)] = value

    def pack_out(t, g, values):
        pair, m = g // 3, g % 3
        even, odd = 2 * pair * slabs + 2 * t, (2 * pair + 1) * slabs + 2 * t
        halves = [mixed(values[2 * i], values[2 * i + 1]) for i in (0, 1)]
        for j in (0, 1):
            first, second = halves[0][j], halves[1][j]
            if m == 1:
                second = pltpu.roll(second, CX, 1)
                pieces[even + j, 2 * ROWS :] = jnp.where(low, first, second)
                pieces[odd + j, 2 * ROWS :] = jnp.where(low, second, first)
            else:
                chunk = (even if m == 0 else odd) + j
                pieces[chunk, :ROWS] = first
                pieces[chunk, ROWS : 2 * ROWS] = second

    def sums(r, tiles, squares):
        beside = beside_of(tiles)
        across, twice = [], []
        for t, g in everywhere:
            value = diag[(r,) + at(t, g)] * tiles[t][g] - beside[t][g]
            applied[(r,) + at(t, g)] = value
            across.append(tiles[t][g] * value)
            twice.append(value * value)
        return add_up(squares), add_up(across), add_up(twice)

    def begin(r):
        center = tiles_of(mean_scratch if packed else mean, r)
        beside = beside_of(center)
        squares = []
        for t, g in everywhere:
            where = at(t, g)
            label = tissue[where]
            shifted = jnp.full(label.shape, 6.0, jnp.float32)
            for c in range(CLASSES):
                shifted = shifted + jnp.where(label == c, kappa[c, r], 0.0)
            diag[(r,) + where] = (design[r] / scale[r]) * factor[where] + shifted
            right = rhs[(r,) + where] + scale[r] * (shifted * center[t][g] - beside[t][g])
            residual[(r,) + where] = right
            direction[(r,) + where] = right
            out[(r,) + where] = jnp.zeros_like(right)
            squares.append(right * right)
            center[t][g] = right
        return sums(r, center, squares)

    def step(r, size, ratio):
        squares, tiles = [], [[None] * groups for _ in range(planes)]
        for t, g in everywhere:
            where = (r,) + at(t, g)
            old = direction[where]
            left = residual[where] - size * applied[where]
            residual[where] = left
            out[where] = out[where] + size * old
            tiles[t][g] = left + ratio * old
            direction[where] = tiles[t][g]
            squares.append(left * left)
        return sums(r, tiles, squares)

    if packed:
        unpack()
    state = tuple(reduced(begin(r)) for r in range(regressors))
    for _ in range(ITERS - 1):
        state = tuple(reduced(step(r, *state[r])) for r in range(regressors))
    for t, g in everywhere:
        values = []
        for r in range(regressors):
            where = (r,) + at(t, g)
            values.append((out[where] + state[r][0] * direction[where]) / scale[r])
            out[where] = values[r]
        if packed:
            pack_out(t, g, values)


def conjugate_gradients(design, kappa, scale, rhs, mean, factor, tissue, packed, slabs):
    smem = pl.BlockSpec(memory_space=pltpu.SMEM)
    vmem = pl.BlockSpec(memory_space=pltpu.VMEM)
    field = pltpu.VMEM(rhs.shape, jnp.float32)
    shapes = [rhs.shape] + [mean.shape] * packed
    return pl.pallas_call(
        functools.partial(cg_kernel, packed=packed, slabs=slabs),
        out_shape=[jax.ShapeDtypeStruct(s, jnp.float32) for s in shapes],
        in_specs=[smem] * 3 + [vmem] * 4,
        out_specs=[vmem] * len(shapes),
        scratch_shapes=[field] * 5,
        compiler_params=pltpu.CompilerParams(vmem_limit_bytes=32 * 2**20),
    )(design, kappa, scale, rhs, mean, factor, tissue)


def exchange(blocks, axis, hops):
    count = lax.axis_size(axis)
    me = lax.axis_index(axis)
    near = [lax.dynamic_index_in_dim(blocks, me ^ k, 0, keepdims=False) for k in range(count)]
    for hop in hops:
        moved = [k for k in range(count) if k & hop == hop] if len(hops) < count - 1 else [hop]
        sent = jnp.stack([near[k] for k in moved])
        got = lax.ppermute(sent, axis, [(i, i ^ hop) for i in range(count)])
        for n, k in enumerate(moved):
            near[k] = got[n]
    out = blocks
    for k in range(1, count):
        out = lax.dynamic_update_index_in_dim(out, near[k], me ^ k, 0)
    return out


def local(
    data_rhs,
    inv_var,
    design,
    keep_mask,
    brain_mask,
    tissue,
    kappa_sq,
    prior_scale,
    mean_field,
    pop_noise,
):
    subjects, slabs = lax.axis_size("subj"), lax.axis_size("slab")
    mine = lax.axis_index("slab")
    total, depth, cells = data_rhs.shape[1:]
    share = mean_field.shape[2]
    part = total // slabs

    packed = fits_packing(part, depth, share, slabs, subjects)
    if packed:
        means = pack(mean_field, subjects, slabs)
    else:
        means = jnp.broadcast_to(mean_field.reshape(1, slabs, part, depth, share), (subjects, slabs, part, depth, share))
        means = means.reshape(subjects * slabs, part, depth, share)
    means, inv_var, tissue = lax.optimization_barrier((means, inv_var, tissue))
    means = lax.all_to_all(means, ("subj", "slab"), 0, 0, tiled=True)
    if not packed:
        means = means.reshape(subjects, slabs, part, depth, share)
        means = jnp.transpose(means, (2, 1, 3, 0, 4)).reshape(part, slabs * depth, cells)

    factor = inv_var * brain_mask.astype(jnp.float32) * keep_mask.astype(jnp.float32)
    planes = jnp.concatenate([factor, tissue.astype(jnp.float32)[None]])
    blocks = jnp.concatenate(
        [
            data_rhs.reshape(slabs, part, depth, cells),
            jnp.broadcast_to(planes[None], (slabs,) + planes.shape),
        ],
        axis=1,
    )
    blocks = exchange(blocks, "slab", [slabs >> n for n in range(1, slabs.bit_length())])
    blocks = jnp.transpose(blocks, (1, 0, 2, 3)).reshape(part + 2, slabs * depth, cells)

    fields, *pieces = conjugate_gradients(
        lax.dynamic_slice_in_dim(design[0], mine * part, part),
        lax.dynamic_slice_in_dim(kappa_sq, mine * part, part, axis=1),
        lax.dynamic_slice_in_dim(prior_scale, mine * part, part),
        blocks[:part],
        means,
        blocks[part],
        blocks[part + 1].astype(jnp.int32),
        packed,
        slabs,
    )

    by_slab = fields.reshape(part, slabs, depth, cells)
    solution = exchange(jnp.transpose(by_slab, (1, 0, 2, 3)), "slab", range(1, slabs)).reshape(1, total, depth, cells)
    if not packed:
        pieces = jnp.transpose(by_slab.reshape(part, slabs, depth, subjects, share), (3, 1, 0, 2, 4))
        pieces = [pieces.reshape(subjects * slabs, part, depth, share)]
    pieces = lax.all_to_all(pieces[0], ("subj", "slab"), 0, 0, tiled=True)
    if packed:
        return solution, finish(pieces, pop_noise, subjects, slabs)
    summed = jnp.sum(pieces.reshape(subjects, total, depth, share), axis=0)
    divisor = subjects + MEAN_PRECISION
    new_mean = summed / divisor + pop_noise / math.sqrt(divisor)
    return solution, new_mean


def solution(mesh):
    in_specs = (
        P("subj", None, "slab", None),
        P("subj", "slab", None),
        P("subj", None),
        P("subj", "slab", None),
        P("slab", None),
        P("slab", None),
        P(),
        P(),
        P(None, "slab", "subj"),
        P(None, "slab", "subj"),
    )
    out_specs = (P("subj", None, "slab", None), P(None, "slab", "subj"))
    return jax.shard_map(local, mesh=mesh, in_specs=in_specs, out_specs=out_specs, check_vma=False)
```

```python
import functools
import math

import jax
import jax.numpy as jnp
from jax import lax
from jax.experimental import pallas as pl
from jax.experimental.pallas import tpu as pltpu
from jax.sharding import PartitionSpec as P

CLASSES = 3
ITERS = 8
CX = 64
LANES = 128
ROWS = 8
DEPTH = 4


MEAN_PRECISION = 1.0


def stencil_matrix(pieces):
    come = lax.broadcasted_iota(jnp.int32, (pieces * LANES, LANES), 0) % LANES
    go = lax.broadcasted_iota(jnp.int32, (pieces * LANES, LANES), 1)
    row = ((come < CX) == (go < CX)) & (abs(come - go) == 1)
    return jnp.where(row | (abs(come - go) == CX), 1.0, 0.0).astype(jnp.bfloat16)


def beside_of(tiles):
    shape = tiles[0][0].shape
    row = lax.broadcasted_iota(jnp.int32, shape, 0)
    low = low_lanes(shape)
    planes, groups = len(tiles), len(tiles[0])
    zero = jnp.zeros(shape, jnp.float32)
    whole = jnp.concatenate([tiles[t][g] for g in range(groups) for t in range(planes)], axis=0)
    coarse = whole.astype(jnp.bfloat16)
    fine = (whole - coarse.astype(jnp.float32)).astype(jnp.bfloat16)
    inside = jnp.dot(
        jnp.concatenate([coarse, fine], axis=1), stencil_matrix(2), preferred_element_type=jnp.float32
    )
    down = [[pltpu.roll(v, 1, 0) for v in line] for line in tiles]
    up = [[pltpu.roll(v, ROWS - 1, 0) for v in line] for line in tiles]
    out = []
    for t in range(planes):
        line = []
        for g in range(groups):
            start = (g * planes + t) * ROWS
            before = tiles[t][g - 1] if g else zero
            after = tiles[t][g + 1] if g + 1 < groups else zero
            total = inside[start : start + ROWS] + pltpu.roll(jnp.where(low, after, before), CX, 1)
            below = down[t - 1][g] if t else zero
            above = up[t + 1][g] if t + 1 < planes else zero
            total = total + (jnp.where(row == 0, below, down[t][g]) + jnp.where(row == ROWS - 1, above, up[t][g]))
            line.append(total)
        out.append(line)
    return out


def mixed(one, two):
    half = lax.broadcasted_iota(jnp.int32, one.shape, 0) < DEPTH
    return jnp.where(half, one, pltpu.roll(two, DEPTH, 0)), jnp.where(half, pltpu.roll(one, DEPTH, 0), two)


def low_lanes(shape):
    return lax.broadcasted_iota(jnp.int32, shape, 1) < CX


def fits_packing(part, depth, share, slabs, subjects):
    return part == 4 and depth == DEPTH and 2 * share == 3 * LANES and slabs % 2 == 0 and subjects % 2 == 0


def pack_kernel(mean, out):
    odd = lax.axis_index("subj") % 2 == 1
    slabs = mean.shape[0] // 4
    for j in range(slabs):
        wide, narrow = [], []
        for k in (4 * j, 4 * j + 2):
            wide.append(jnp.concatenate([mean[k, :, :LANES], mean[k + 1, :, :LANES]], axis=0))
            rest = jnp.concatenate([mean[k, :, LANES:], mean[k + 1, :, LANES:]], axis=0)
            narrow.append(jnp.concatenate([rest, rest], axis=1))
        low = low_lanes(wide[0].shape)
        turned = [pltpu.roll(w, CX, 1) for w in wide]
        rows = [jnp.where(odd, jnp.where(low, turned[i], narrow[i]), wide[i]) for i in (0, 1)]
        rows.append(jnp.where(odd, jnp.where(low, wide[1], turned[0]), jnp.where(low, narrow[0], narrow[1])))
        for s in range(out.shape[0] // slabs):
            for i in range(3):
                out[s * slabs + j, ROWS * i : ROWS * (i + 1)] = rows[i]


def pack(mean, subjects, slabs):
    return pl.pallas_call(
        pack_kernel,
        out_shape=jax.ShapeDtypeStruct((subjects * slabs, 3 * ROWS, LANES), jnp.float32),
        in_specs=[pl.BlockSpec(memory_space=pltpu.VMEM)],
        out_specs=pl.BlockSpec(memory_space=pltpu.VMEM),
        compiler_params=pltpu.CompilerParams(vmem_limit_bytes=4 * 2**20),
    )(mean)


def finish_kernel(pieces, noise, *refs, subjects):
    *blocks, new_mean, fields, out, sems, out_sem = refs
    slabs, part = len(blocks), blocks[0].shape[0]
    me = lax.axis_index("slab")
    odd = lax.axis_index("subj") % 2 == 1
    copies = []
    for k, block in enumerate(blocks):
        target = fields.at[0, pl.ds((me ^ k) * part, part)]
        copies.append(pltpu.make_async_copy(block, target, sems.at[k]))
        copies[k].start()
    divisor = subjects + MEAN_PRECISION
    for j in range(slabs):
        rows = []
        for i in range(3):
            total = pieces[j, ROWS * i : ROWS * (i + 1)]
            for s in range(1, subjects):
                total = total + pieces[s * slabs + j, ROWS * i : ROWS * (i + 1)]
            rows.append(total / divisor)
        low = low_lanes(rows[0].shape)
        turned = [pltpu.roll(v, CX, 1) for v in rows]
        for i in (0, 1):
            mid = (rows[2], turned[2])
            wide = jnp.where(odd, jnp.where(low, mid[1 - i], turned[i]), rows[i])
            narrow = jnp.where(odd, turned[i], mid[i])
            for n in (0, 1):
                k, here = 4 * j + 2 * i + n, slice(DEPTH * n, DEPTH * (n + 1))
                out[k, :, :LANES] = wide[here] + noise[k, :, :LANES] / math.sqrt(divisor)
                out[k, :, LANES:] = narrow[here, :CX] + noise[k, :, LANES:] / math.sqrt(divisor)
    copies.append(pltpu.make_async_copy(out, new_mean, out_sem))
    copies[-1].start()
    for copy in copies:
        copy.wait()


def finish(pieces, noise, blocks, subjects):
    vmem = pl.BlockSpec(memory_space=pltpu.VMEM)
    anywhere = pl.BlockSpec(memory_space=pl.ANY)
    slabs, (part, depth, cells) = len(blocks), blocks[0].shape
    return pl.pallas_call(
        functools.partial(finish_kernel, subjects=subjects),
        out_shape=[
            jax.ShapeDtypeStruct(noise.shape, jnp.float32),
            jax.ShapeDtypeStruct((1, slabs * part, depth, cells), jnp.float32),
        ],
        in_specs=[vmem] * 2 + [anywhere] * slabs,
        out_specs=[anywhere] * 2,
        scratch_shapes=[
            pltpu.VMEM(noise.shape, jnp.float32),
            pltpu.SemaphoreType.DMA((slabs,)),
            pltpu.SemaphoreType.DMA,
        ],
        compiler_params=pltpu.CompilerParams(vmem_limit_bytes=4 * 2**20),
    )(pieces, noise, *blocks)


def cg_kernel(table, rhs, mean, factor, tissue, *refs, packed, slabs):
    *outs, diag, direction, residual, applied, mean_scratch, total = refs
    blocks, pieces = outs[:-1], outs[-1]
    regressors, depth, cells = rhs.shape
    planes, groups = depth // ROWS, cells // LANES
    everywhere = [(t, g) for t in range(planes) for g in range(groups)]
    low = low_lanes((ROWS, LANES))

    def at(t, g):
        return pl.ds(t * ROWS, ROWS), pl.ds(g * LANES, LANES)

    def tiles_of(ref, r):
        return [[ref[(r,) + at(t, g)] for g in range(groups)] for t in range(planes)]

    def add_up(parts):
        while len(parts) > 1:
            parts = [sum(parts[i : i + 2][1:], parts[i]) for i in range(0, len(parts), 2)]
        return parts[0]

    def reduced(parts):
        own, across, twice = (jnp.sum(p, axis=(0, 1), keepdims=True) for p in parts)
        size = own / across
        return size, size * (twice / across) - 1.0

    def unpack():
        for t, g in everywhere:
            pair, m = g // 3, g % 3
            even, odd = 2 * pair * slabs + 2 * t, (2 * pair + 1) * slabs + 2 * t
            for i in (0, 1):
                two = []
                for j in (0, 1):
                    if m == 1:
                        first, second = mean[even + j, 2 * ROWS :], mean[odd + j, 2 * ROWS :]
                        if i == 0:
                            two.append(jnp.where(low, first, second))
                        else:
                            two.append(pltpu.roll(jnp.where(low, second, first), CX, 1))
                    else:
                        two.append(mean[(even if m == 0 else odd) + j, ROWS * i : ROWS * (i + 1)])
                for n, value in enumerate(mixed(*two)):
                    mean_scratch[(2 * i + n,) + at(t, g)] = value

    def pack_out(t, g, values):
        pair, m = g // 3, g % 3
        even, odd = 2 * pair * slabs + 2 * t, (2 * pair + 1) * slabs + 2 * t
        halves = [mixed(values[2 * i], values[2 * i + 1]) for i in (0, 1)]
        for j in (0, 1):
            first, second = halves[0][j], halves[1][j]
            if m == 1:
                second = pltpu.roll(second, CX, 1)
                pieces[even + j, 2 * ROWS :] = jnp.where(low, first, second)
                pieces[odd + j, 2 * ROWS :] = jnp.where(low, second, first)
            else:
                chunk = (even if m == 0 else odd) + j
                pieces[chunk, :ROWS] = first
                pieces[chunk, ROWS : 2 * ROWS] = second

    def sums(r, tiles, squares):
        beside = beside_of(tiles)
        across, twice = [], []
        for t, g in everywhere:
            value = diag[(r,) + at(t, g)] * tiles[t][g] - beside[t][g]
            applied[(r,) + at(t, g)] = value
            across.append(tiles[t][g] * value)
            twice.append(value * value)
        return add_up(squares), add_up(across), add_up(twice)

    def begin(r):
        ratio, scale, *kappas = (table[r, i : i + 1] for i in range(2 + CLASSES))
        center = tiles_of(mean_scratch if packed else mean, r)
        beside = beside_of(center)
        squares = []
        for t, g in everywhere:
            where = at(t, g)
            label = tissue[where]
            shifted = jnp.full(label.shape, 6.0, jnp.float32)
            for c in range(CLASSES):
                shifted = shifted + jnp.where(label == c, kappas[c], 0.0)
            diag[(r,) + where] = ratio * factor[where] + shifted
            right = rhs[(r,) + where] + scale * (shifted * center[t][g] - beside[t][g])
            residual[(r,) + where] = right
            direction[(r,) + where] = right
            total[(r,) + where] = jnp.zeros_like(right)
            squares.append(right * right)
            center[t][g] = right
        return sums(r, center, squares)

    def step(r, size, ratio):
        squares, tiles = [], [[None] * groups for _ in range(planes)]
        for t, g in everywhere:
            where = (r,) + at(t, g)
            old = direction[where]
            left = residual[where] - size * applied[where]
            residual[where] = left
            total[where] = total[where] + size * old
            tiles[t][g] = left + ratio * old
            direction[where] = tiles[t][g]
            squares.append(left * left)
        return sums(r, tiles, squares)

    if packed:
        unpack()
    state = tuple(reduced(begin(r)) for r in range(regressors))
    for _ in range(ITERS - 1):
        state = tuple(reduced(step(r, *state[r])) for r in range(regressors))
    for t, g in everywhere:
        values = []
        for r in range(regressors):
            where = (r,) + at(t, g)
            values.append((total[where] + state[r][0] * direction[where]) / table[r, 1:2])
            (total if packed else outs[0])[where] = values[r]
        if packed:
            pack_out(t, g, values)
    if packed:
        me = lax.axis_index("slab")
        for m in range(slabs):

            @pl.when(me == m)
            def _():
                for j in range(slabs):
                    for r in range(regressors):
                        blocks[j ^ m][r] = total[r, DEPTH * j : DEPTH * (j + 1)]


def conjugate_gradients(design, kappa, scale, rhs, mean, factor, tissue, packed, slabs):
    vmem = pl.BlockSpec(memory_space=pltpu.VMEM)
    table = jnp.concatenate([(design / scale)[None], scale[None], kappa])
    table = jnp.pad(table, ((0, ROWS - 2 - CLASSES), (0, 0)))
    table = jnp.broadcast_to(jnp.transpose(table)[:, :, None], (scale.shape[0], ROWS, LANES))
    field = pltpu.VMEM(rhs.shape, jnp.float32)
    part, depth, cells = rhs.shape
    shapes = [(part, depth // slabs, cells)] * slabs + [mean.shape] if packed else [rhs.shape]
    return pl.pallas_call(
        functools.partial(cg_kernel, packed=packed, slabs=slabs),
        out_shape=[jax.ShapeDtypeStruct(s, jnp.float32) for s in shapes],
        in_specs=[vmem] * 5,
        out_specs=[vmem] * len(shapes),
        scratch_shapes=[field] * 6,
        compiler_params=pltpu.CompilerParams(vmem_limit_bytes=32 * 2**20),
    )(table, rhs, mean, factor, tissue)


def nearest_first(blocks, axis):
    me = lax.axis_index(axis)
    return [lax.dynamic_index_in_dim(blocks, me ^ k, 0, keepdims=False) for k in range(lax.axis_size(axis))]


def in_order(near, axis):
    me = lax.axis_index(axis)
    out = jnp.stack(near)
    for k in range(len(near)):
        out = lax.dynamic_update_index_in_dim(out, near[k], me ^ k, 0)
    return out


def swap(block, axis, k):
    return lax.ppermute(block, axis, [(i, i ^ k) for i in range(lax.axis_size(axis))])


def direct(near, axis):
    return [near[0]] + [swap(near[k], axis, k) for k in range(1, len(near))]


def hop(near, axis, bit):
    near = list(near)
    moved = [k for k in range(len(near)) if k & bit]
    got = swap(jnp.stack([near[k] for k in moved]), axis, bit)
    for n, k in enumerate(moved):
        near[k] = got[n]
    return near


def local(
    data_rhs,
    inv_var,
    design,
    keep_mask,
    brain_mask,
    tissue,
    kappa_sq,
    prior_scale,
    mean_field,
    pop_noise,
):
    subjects, slabs = lax.axis_size("subj"), lax.axis_size("slab")
    mine = lax.axis_index("slab")
    total, depth, cells = data_rhs.shape[1:]
    share = mean_field.shape[2]
    part = total // slabs

    packed = fits_packing(part, depth, share, slabs, subjects)
    if packed:
        means = pack(mean_field, subjects, slabs)
    else:
        means = jnp.broadcast_to(mean_field.reshape(1, slabs, part, depth, share), (subjects, slabs, part, depth, share))
        means = means.reshape(subjects * slabs, part, depth, share)
    means = lax.all_to_all(means, ("subj", "slab"), 0, 0, tiled=True)
    if not packed:
        means = means.reshape(subjects, slabs, part, depth, share)
        means = jnp.transpose(means, (2, 1, 3, 0, 4)).reshape(part, slabs * depth, cells)

    bits = [slabs >> n for n in range(1, slabs.bit_length())]
    near = nearest_first(data_rhs.reshape(slabs, part, depth, cells), "slab")
    near = hop(near, "slab", bits[0])
    near, inv_var = lax.optimization_barrier((near, inv_var))
    factor = inv_var * brain_mask.astype(jnp.float32) * keep_mask.astype(jnp.float32)
    planes = jnp.concatenate([factor, tissue.astype(jnp.float32)[None]])
    for bit in bits[1:]:
        near = hop(near, "slab", bit)
    planes = in_order(direct([planes] * slabs, "slab"), "slab")
    blocks = in_order(near, "slab")
    blocks = jnp.transpose(blocks, (1, 0, 2, 3)).reshape(part, slabs * depth, cells)
    planes = jnp.transpose(planes, (1, 0, 2, 3)).reshape(2, slabs * depth, cells)

    fields = conjugate_gradients(
        lax.dynamic_slice_in_dim(design[0], mine * part, part),
        lax.dynamic_slice_in_dim(kappa_sq, mine * part, part, axis=1),
        lax.dynamic_slice_in_dim(prior_scale, mine * part, part),
        blocks,
        means,
        planes[0],
        planes[1].astype(jnp.int32),
        packed,
        slabs,
    )

    if packed:
        *near, pieces = fields
        pieces = lax.all_to_all(pieces, ("subj", "slab"), 0, 0, tiled=True)
        new_mean, solution = finish(pieces, pop_noise, direct(near, "slab"), subjects)
        return solution, new_mean
    by_slab = fields[0].reshape(part, slabs, depth, cells)
    near = nearest_first(jnp.transpose(by_slab, (1, 0, 2, 3)), "slab")
    solution = in_order(direct(near, "slab"), "slab").reshape(1, total, depth, cells)
    pieces = jnp.transpose(by_slab.reshape(part, slabs, depth, subjects, share), (3, 1, 0, 2, 4))
    pieces = pieces.reshape(subjects * slabs, part, depth, share)
    pieces = lax.all_to_all(pieces, ("subj", "slab"), 0, 0, tiled=True)
    summed = jnp.sum(pieces.reshape(subjects, total, depth, share), axis=0)
    divisor = subjects + MEAN_PRECISION
    new_mean = summed / divisor + pop_noise / math.sqrt(divisor)
    return solution, new_mean


def solution(mesh):
    in_specs = (
        P("subj", None, "slab", None),
        P("subj", "slab", None),
        P("subj", None),
        P("subj", "slab", None),
        P("slab", None),
        P("slab", None),
        P(),
        P(),
        P(None, "slab", "subj"),
        P(None, "slab", "subj"),
    )
    out_specs = (P("subj", None, "slab", None), P(None, "slab", "subj"))
    return jax.shard_map(local, mesh=mesh, in_specs=in_specs, out_specs=out_specs, check_vma=False)
```

```python
import functools
import math

import jax
import jax.numpy as jnp
from jax import lax
from jax.experimental import pallas as pl
from jax.experimental.pallas import tpu as pltpu
from jax.sharding import PartitionSpec as P

CLASSES = 3
ITERS = 8
CX = 64
LANES = 128
ROWS = 8
DEPTH = 4


MEAN_PRECISION = 1.0


def inner_neighbours(lane):
    x = lane % CX
    return jnp.where((x == 0) | (x == CX - 1), 2.0, 3.0)


def stencil_matrix(pieces):
    come = lax.broadcasted_iota(jnp.int32, (pieces * LANES, LANES), 0) % LANES
    go = lax.broadcasted_iota(jnp.int32, (pieces * LANES, LANES), 1)
    row = ((come < CX) == (go < CX)) & (abs(come - go) == 1)
    near = jnp.where(row | (abs(come - go) == CX), 1.0, 0.0)
    inner = jnp.where(come == go, -inner_neighbours(go), near)
    turned = jnp.where(abs(come - go) == CX, 1.0, 0.0)
    return jnp.concatenate([inner, turned], axis=1).astype(jnp.bfloat16)


def beside_of(tiles):
    shape = tiles[0][0].shape
    row = lax.broadcasted_iota(jnp.int32, shape, 0)
    low = low_lanes(shape)
    planes, groups = len(tiles), len(tiles[0])
    zero = jnp.zeros(shape, jnp.float32)
    whole = jnp.concatenate([tiles[t][g] for g in range(groups) for t in range(planes)], axis=0)
    coarse = whole.astype(jnp.bfloat16)
    rest = whole - coarse.astype(jnp.float32)
    fine = rest.astype(jnp.bfloat16)
    last = (rest - fine.astype(jnp.float32)).astype(jnp.bfloat16)
    inside = jnp.dot(
        jnp.concatenate([coarse, fine, last], axis=1), stencil_matrix(3), preferred_element_type=jnp.float32
    )
    down = [[pltpu.roll(v, 1, 0) for v in line] for line in tiles]
    up = [[pltpu.roll(v, ROWS - 1, 0) for v in line] for line in tiles]
    out = []
    for t in range(planes):
        line = []
        for g in range(groups):
            start = (g * planes + t) * ROWS
            before = inside[start - planes * ROWS :][:ROWS, LANES:] if g else zero
            after = inside[start + planes * ROWS :][:ROWS, LANES:] if g + 1 < groups else zero
            total = inside[start : start + ROWS, :LANES] + jnp.where(low, before, after)
            below = down[t - 1][g] if t else zero
            above = up[t + 1][g] if t + 1 < planes else zero
            total = total + (jnp.where(row == 0, below, down[t][g]) + jnp.where(row == ROWS - 1, above, up[t][g]))
            line.append(total)
        out.append(line)
    return out


def mixed(one, two):
    half = lax.broadcasted_iota(jnp.int32, one.shape, 0) < DEPTH
    return jnp.where(half, one, pltpu.roll(two, DEPTH, 0)), jnp.where(half, pltpu.roll(one, DEPTH, 0), two)


def low_lanes(shape):
    return lax.broadcasted_iota(jnp.int32, shape, 1) < CX


def fits_packing(part, depth, share, slabs, subjects):
    return part == 4 and depth == DEPTH and 2 * share == 3 * LANES and slabs % 2 == 0 and subjects % 2 == 0


def pack_kernel(mean, out):
    odd = lax.axis_index("subj") % 2 == 1
    slabs = mean.shape[0] // 4
    for j in range(slabs):
        wide, narrow = [], []
        for k in (4 * j, 4 * j + 2):
            wide.append(jnp.concatenate([mean[k, :, :LANES], mean[k + 1, :, :LANES]], axis=0))
            rest = jnp.concatenate([mean[k, :, LANES:], mean[k + 1, :, LANES:]], axis=0)
            narrow.append(jnp.concatenate([rest, rest], axis=1))
        low = low_lanes(wide[0].shape)
        turned = [pltpu.roll(w, CX, 1) for w in wide]
        rows = [jnp.where(odd, jnp.where(low, turned[i], narrow[i]), wide[i]) for i in (0, 1)]
        rows.append(jnp.where(odd, jnp.where(low, wide[1], turned[0]), jnp.where(low, narrow[0], narrow[1])))
        for s in range(out.shape[0] // slabs):
            for i in range(3):
                out[s * slabs + j, ROWS * i : ROWS * (i + 1)] = rows[i]


def pack(mean, subjects, slabs):
    return pl.pallas_call(
        pack_kernel,
        out_shape=jax.ShapeDtypeStruct((subjects * slabs, 3 * ROWS, LANES), jnp.float32),
        in_specs=[pl.BlockSpec(memory_space=pltpu.VMEM)],
        out_specs=pl.BlockSpec(memory_space=pltpu.VMEM),
        compiler_params=pltpu.CompilerParams(vmem_limit_bytes=4 * 2**20),
    )(mean)


def finish_kernel(pieces, noise, *refs, subjects):
    *blocks, new_mean, fields, out, sems, out_sem = refs
    slabs, part = len(blocks), blocks[0].shape[0]
    me = lax.axis_index("slab")
    odd = lax.axis_index("subj") % 2 == 1
    copies = []
    for k, block in enumerate(blocks):
        target = fields.at[0, pl.ds((me ^ k) * part, part)]
        copies.append(pltpu.make_async_copy(block, target, sems.at[k]))
        copies[k].start()
    divisor = subjects + MEAN_PRECISION
    for j in range(slabs):
        rows = []
        for i in range(3):
            total = pieces[j, ROWS * i : ROWS * (i + 1)]
            for s in range(1, subjects):
                total = total + pieces[s * slabs + j, ROWS * i : ROWS * (i + 1)]
            rows.append(total / divisor)
        low = low_lanes(rows[0].shape)
        turned = [pltpu.roll(v, CX, 1) for v in rows]
        for i in (0, 1):
            mid = (rows[2], turned[2])
            wide = jnp.where(odd, jnp.where(low, mid[1 - i], turned[i]), rows[i])
            narrow = jnp.where(odd, turned[i], mid[i])
            for n in (0, 1):
                k, here = 4 * j + 2 * i + n, slice(DEPTH * n, DEPTH * (n + 1))
                out[k, :, :LANES] = wide[here] + noise[k, :, :LANES] / math.sqrt(divisor)
                out[k, :, LANES:] = narrow[here, :CX] + noise[k, :, LANES:] / math.sqrt(divisor)
    copies.append(pltpu.make_async_copy(out, new_mean, out_sem))
    copies[-1].start()
    for copy in copies:
        copy.wait()


def finish(pieces, noise, blocks, subjects):
    vmem = pl.BlockSpec(memory_space=pltpu.VMEM)
    anywhere = pl.BlockSpec(memory_space=pl.ANY)
    slabs, (part, depth, cells) = len(blocks), blocks[0].shape
    return pl.pallas_call(
        functools.partial(finish_kernel, subjects=subjects),
        out_shape=[
            jax.ShapeDtypeStruct(noise.shape, jnp.float32),
            jax.ShapeDtypeStruct((1, slabs * part, depth, cells), jnp.float32),
        ],
        in_specs=[vmem] * 2 + [anywhere] * slabs,
        out_specs=[anywhere] * 2,
        scratch_shapes=[
            pltpu.VMEM(noise.shape, jnp.float32),
            pltpu.SemaphoreType.DMA((slabs,)),
            pltpu.SemaphoreType.DMA,
        ],
        compiler_params=pltpu.CompilerParams(vmem_limit_bytes=4 * 2**20),
    )(pieces, noise, *blocks)


def cg_kernel(table, rhs, mean, factor, tissue, *refs, packed, slabs):
    *outs, diag, direction, residual, applied, mean_scratch, total = refs
    blocks, pieces = outs[:-1], outs[-1]
    regressors, depth, cells = rhs.shape
    planes, groups = depth // ROWS, cells // LANES
    everywhere = [(t, g) for t in range(planes) for g in range(groups)]
    low = low_lanes((ROWS, LANES))

    def at(t, g):
        return pl.ds(t * ROWS, ROWS), pl.ds(g * LANES, LANES)

    def tiles_of(ref, r):
        return [[ref[(r,) + at(t, g)] for g in range(groups)] for t in range(planes)]

    def add_up(parts):
        while len(parts) > 1:
            parts = [sum(parts[i : i + 2][1:], parts[i]) for i in range(0, len(parts), 2)]
        return parts[0]

    def reduced(parts):
        own, across, twice = (jnp.sum(p, axis=(0, 1), keepdims=True) for p in parts)
        size = own / across
        return size, size * (twice / across) - 1.0

    def unpack():
        for t, g in everywhere:
            pair, m = g // 3, g % 3
            even, odd = 2 * pair * slabs + 2 * t, (2 * pair + 1) * slabs + 2 * t
            for i in (0, 1):
                two = []
                for j in (0, 1):
                    if m == 1:
                        first, second = mean[even + j, 2 * ROWS :], mean[odd + j, 2 * ROWS :]
                        if i == 0:
                            two.append(jnp.where(low, first, second))
                        else:
                            two.append(pltpu.roll(jnp.where(low, second, first), CX, 1))
                    else:
                        two.append(mean[(even if m == 0 else odd) + j, ROWS * i : ROWS * (i + 1)])
                for n, value in enumerate(mixed(*two)):
                    mean_scratch[(2 * i + n,) + at(t, g)] = value

    def pack_out(t, g, values):
        pair, m = g // 3, g % 3
        even, odd = 2 * pair * slabs + 2 * t, (2 * pair + 1) * slabs + 2 * t
        halves = [mixed(values[2 * i], values[2 * i + 1]) for i in (0, 1)]
        for j in (0, 1):
            first, second = halves[0][j], halves[1][j]
            if m == 1:
                second = pltpu.roll(second, CX, 1)
                pieces[even + j, 2 * ROWS :] = jnp.where(low, first, second)
                pieces[odd + j, 2 * ROWS :] = jnp.where(low, second, first)
            else:
                chunk = (even if m == 0 else odd) + j
                pieces[chunk, :ROWS] = first
                pieces[chunk, ROWS : 2 * ROWS] = second

    def sums(r, tiles, squares):
        beside = beside_of(tiles)
        across, twice = [], []
        for t, g in everywhere:
            value = diag[(r,) + at(t, g)] * tiles[t][g] - beside[t][g]
            applied[(r,) + at(t, g)] = value
            across.append(tiles[t][g] * value)
            twice.append(value * value)
        return add_up(squares), add_up(across), add_up(twice)

    def begin(r):
        ratio, scale, *kappas = (table[r, i : i + 1] for i in range(2 + CLASSES))
        center = tiles_of(mean_scratch if packed else mean, r)
        beside = beside_of(center)
        squares = []
        for t, g in everywhere:
            where = at(t, g)
            label = tissue[where]
            shifted = 6.0 - inner_neighbours(lax.broadcasted_iota(jnp.int32, label.shape, 1))
            for c in range(CLASSES):
                shifted = shifted + jnp.where(label == c, kappas[c], 0.0)
            diag[(r,) + where] = ratio * factor[where] + shifted
            right = rhs[(r,) + where] + scale * (shifted * center[t][g] - beside[t][g])
            residual[(r,) + where] = right
            direction[(r,) + where] = right
            total[(r,) + where] = jnp.zeros_like(right)
            squares.append(right * right)
            center[t][g] = right
        return sums(r, center, squares)

    def step(r, size, ratio):
        squares, tiles = [], [[None] * groups for _ in range(planes)]
        for t, g in everywhere:
            where = (r,) + at(t, g)
            old = direction[where]
            left = residual[where] - size * applied[where]
            residual[where] = left
            total[where] = total[where] + size * old
            tiles[t][g] = left + ratio * old
            direction[where] = tiles[t][g]
            squares.append(left * left)
        return sums(r, tiles, squares)

    if packed:
        unpack()
    state = tuple(reduced(begin(r)) for r in range(regressors))
    for _ in range(ITERS - 1):
        state = tuple(reduced(step(r, *state[r])) for r in range(regressors))
    for t, g in everywhere:
        values = []
        for r in range(regressors):
            where = (r,) + at(t, g)
            values.append((total[where] + state[r][0] * direction[where]) / table[r, 1:2])
            (total if packed else outs[0])[where] = values[r]
        if packed:
            pack_out(t, g, values)
    if packed:
        me = lax.axis_index("slab")
        for m in range(slabs):

            @pl.when(me == m)
            def _():
                for j in range(slabs):
                    for r in range(regressors):
                        blocks[j ^ m][r] = total[r, DEPTH * j : DEPTH * (j + 1)]


def conjugate_gradients(design, kappa, scale, rhs, mean, factor, tissue, packed, slabs):
    vmem = pl.BlockSpec(memory_space=pltpu.VMEM)
    table = jnp.concatenate([(design / scale)[None], scale[None], kappa])
    table = jnp.pad(table, ((0, ROWS - 2 - CLASSES), (0, 0)))
    table = jnp.broadcast_to(jnp.transpose(table)[:, :, None], (scale.shape[0], ROWS, LANES))
    field = pltpu.VMEM(rhs.shape, jnp.float32)
    part, depth, cells = rhs.shape
    shapes = [(part, depth // slabs, cells)] * slabs + [mean.shape] if packed else [rhs.shape]
    return pl.pallas_call(
        functools.partial(cg_kernel, packed=packed, slabs=slabs),
        out_shape=[jax.ShapeDtypeStruct(s, jnp.float32) for s in shapes],
        in_specs=[vmem] * 5,
        out_specs=[vmem] * len(shapes),
        scratch_shapes=[field] * 6,
        compiler_params=pltpu.CompilerParams(vmem_limit_bytes=32 * 2**20),
    )(table, rhs, mean, factor, tissue)


def nearest_first(blocks, axis):
    me = lax.axis_index(axis)
    return [lax.dynamic_index_in_dim(blocks, me ^ k, 0, keepdims=False) for k in range(lax.axis_size(axis))]


def in_order(near, axis):
    me = lax.axis_index(axis)
    out = jnp.stack(near)
    for k in range(len(near)):
        out = lax.dynamic_update_index_in_dim(out, near[k], me ^ k, 0)
    return out


def swap(block, axis, k):
    return lax.ppermute(block, axis, [(i, i ^ k) for i in range(lax.axis_size(axis))])


def direct(near, axis):
    return [near[0]] + [swap(near[k], axis, k) for k in range(1, len(near))]


def hop(near, axis, bit):
    near = list(near)
    moved = [k for k in range(len(near)) if k & bit]
    got = swap(jnp.stack([near[k] for k in moved]), axis, bit)
    for n, k in enumerate(moved):
        near[k] = got[n]
    return near


def local(
    data_rhs,
    inv_var,
    design,
    keep_mask,
    brain_mask,
    tissue,
    kappa_sq,
    prior_scale,
    mean_field,
    pop_noise,
):
    subjects, slabs = lax.axis_size("subj"), lax.axis_size("slab")
    mine = lax.axis_index("slab")
    total, depth, cells = data_rhs.shape[1:]
    share = mean_field.shape[2]
    part = total // slabs

    packed = fits_packing(part, depth, share, slabs, subjects)
    if packed:
        means = pack(mean_field, subjects, slabs)
    else:
        means = jnp.broadcast_to(mean_field.reshape(1, slabs, part, depth, share), (subjects, slabs, part, depth, share))
        means = means.reshape(subjects * slabs, part, depth, share)
    means = lax.all_to_all(means, ("subj", "slab"), 0, 0, tiled=True)
    if not packed:
        means = means.reshape(subjects, slabs, part, depth, share)
        means = jnp.transpose(means, (2, 1, 3, 0, 4)).reshape(part, slabs * depth, cells)

    bits = [slabs >> n for n in range(1, slabs.bit_length())]
    near = nearest_first(data_rhs.reshape(slabs, part, depth, cells), "slab")
    near = hop(near, "slab", bits[0])
    near, inv_var = lax.optimization_barrier((near, inv_var))
    factor = inv_var * brain_mask.astype(jnp.float32) * keep_mask.astype(jnp.float32)
    planes = jnp.concatenate([factor, tissue.astype(jnp.float32)[None]])
    for bit in bits[1:]:
        near = hop(near, "slab", bit)
    planes = in_order(direct([planes] * slabs, "slab"), "slab")
    blocks = in_order(near, "slab")
    blocks = jnp.transpose(blocks, (1, 0, 2, 3)).reshape(part, slabs * depth, cells)
    planes = jnp.transpose(planes, (1, 0, 2, 3)).reshape(2, slabs * depth, cells)

    fields = conjugate_gradients(
        lax.dynamic_slice_in_dim(design[0], mine * part, part),
        lax.dynamic_slice_in_dim(kappa_sq, mine * part, part, axis=1),
        lax.dynamic_slice_in_dim(prior_scale, mine * part, part),
        blocks,
        means,
        planes[0],
        planes[1].astype(jnp.int32),
        packed,
        slabs,
    )

    if packed:
        *near, pieces = fields
        pieces = lax.all_to_all(pieces, ("subj", "slab"), 0, 0, tiled=True)
        new_mean, solution = finish(pieces, pop_noise, direct(near, "slab"), subjects)
        return solution, new_mean
    by_slab = fields[0].reshape(part, slabs, depth, cells)
    near = nearest_first(jnp.transpose(by_slab, (1, 0, 2, 3)), "slab")
    solution = in_order(direct(near, "slab"), "slab").reshape(1, total, depth, cells)
    pieces = jnp.transpose(by_slab.reshape(part, slabs, depth, subjects, share), (3, 1, 0, 2, 4))
    pieces = pieces.reshape(subjects * slabs, part, depth, share)
    pieces = lax.all_to_all(pieces, ("subj", "slab"), 0, 0, tiled=True)
    summed = jnp.sum(pieces.reshape(subjects, total, depth, share), axis=0)
    divisor = subjects + MEAN_PRECISION
    new_mean = summed / divisor + pop_noise / math.sqrt(divisor)
    return solution, new_mean


def solution(mesh):
    in_specs = (
        P("subj", None, "slab", None),
        P("subj", "slab", None),
        P("subj", None),
        P("subj", "slab", None),
        P("slab", None),
        P("slab", None),
        P(),
        P(),
        P(None, "slab", "subj"),
        P(None, "slab", "subj"),
    )
    out_specs = (P("subj", None, "slab", None), P(None, "slab", "subj"))
    return jax.shard_map(local, mesh=mesh, in_specs=in_specs, out_specs=out_specs, check_vma=False)
```

```python
import functools
import math

import jax
import jax.numpy as jnp
from jax import lax
from jax.experimental import pallas as pl
from jax.experimental.pallas import tpu as pltpu
from jax.sharding import PartitionSpec as P

CLASSES = 3
ITERS = 8
CX = 64
LANES = 128
ROWS = 8
DEPTH = 4


MEAN_PRECISION = 1.0


def inner_neighbours(lane):
    x = lane % CX
    return jnp.where((x == 0) | (x == CX - 1), 2.0, 3.0)


def stencil_matrix(pieces):
    come = lax.broadcasted_iota(jnp.int32, (pieces * LANES, LANES), 0) % LANES
    go = lax.broadcasted_iota(jnp.int32, (pieces * LANES, LANES), 1)
    row = ((come < CX) == (go < CX)) & (abs(come - go) == 1)
    near = jnp.where(row | (abs(come - go) == CX), 1.0, 0.0)
    return jnp.where(come == go, -inner_neighbours(go), near).astype(jnp.bfloat16)


def beside_of(tiles, count):
    shape = tiles[0][0].shape
    row = lax.broadcasted_iota(jnp.int32, shape, 0)
    low = low_lanes(shape)
    planes, groups = len(tiles), len(tiles[0])
    zero = jnp.zeros(shape, jnp.float32)
    rest = jnp.concatenate([tiles[t][g] for g in range(groups) for t in range(planes)], axis=0)
    pieces = []
    for _ in range(count):
        pieces.append(rest.astype(jnp.bfloat16))
        if len(pieces) < count:
            rest = rest - pieces[-1].astype(jnp.float32)
    inside = jnp.dot(
        jnp.concatenate(pieces, axis=1), stencil_matrix(count), preferred_element_type=jnp.float32
    )
    down = [[pltpu.roll(v, 1, 0) for v in line] for line in tiles]
    up = [[pltpu.roll(v, ROWS - 1, 0) for v in line] for line in tiles]
    out = []
    for t in range(planes):
        line = []
        for g in range(groups):
            start = (g * planes + t) * ROWS
            before = tiles[t][g - 1] if g else zero
            after = tiles[t][g + 1] if g + 1 < groups else zero
            total = inside[start : start + ROWS] + pltpu.roll(jnp.where(low, after, before), CX, 1)
            below = down[t - 1][g] if t else zero
            above = up[t + 1][g] if t + 1 < planes else zero
            total = total + (jnp.where(row == 0, below, down[t][g]) + jnp.where(row == ROWS - 1, above, up[t][g]))
            line.append(total)
        out.append(line)
    return out


def mixed(one, two):
    half = lax.broadcasted_iota(jnp.int32, one.shape, 0) < DEPTH
    return jnp.where(half, one, pltpu.roll(two, DEPTH, 0)), jnp.where(half, pltpu.roll(one, DEPTH, 0), two)


def low_lanes(shape):
    return lax.broadcasted_iota(jnp.int32, shape, 1) < CX


def fits_packing(part, depth, share, slabs, subjects):
    return part == 4 and depth == DEPTH and 2 * share == 3 * LANES and slabs % 2 == 0 and subjects % 2 == 0


def pack_kernel(mean, out):
    odd = lax.axis_index("subj") % 2 == 1
    slabs = mean.shape[0] // 4
    for j in range(slabs):
        wide, narrow = [], []
        for k in (4 * j, 4 * j + 2):
            wide.append(jnp.concatenate([mean[k, :, :LANES], mean[k + 1, :, :LANES]], axis=0))
            rest = jnp.concatenate([mean[k, :, LANES:], mean[k + 1, :, LANES:]], axis=0)
            narrow.append(jnp.concatenate([rest, rest], axis=1))
        low = low_lanes(wide[0].shape)
        turned = [pltpu.roll(w, CX, 1) for w in wide]
        rows = [jnp.where(odd, jnp.where(low, turned[i], narrow[i]), wide[i]) for i in (0, 1)]
        rows.append(jnp.where(odd, jnp.where(low, wide[1], turned[0]), jnp.where(low, narrow[0], narrow[1])))
        for s in range(out.shape[0] // slabs):
            for i in range(3):
                out[s * slabs + j, ROWS * i : ROWS * (i + 1)] = rows[i]


def pack(mean, subjects, slabs):
    return pl.pallas_call(
        pack_kernel,
        out_shape=jax.ShapeDtypeStruct((subjects * slabs, 3 * ROWS, LANES), jnp.float32),
        in_specs=[pl.BlockSpec(memory_space=pltpu.VMEM)],
        out_specs=pl.BlockSpec(memory_space=pltpu.VMEM),
        compiler_params=pltpu.CompilerParams(vmem_limit_bytes=4 * 2**20),
    )(mean)


def finish_kernel(pieces, noise, *refs, subjects):
    *blocks, new_mean, fields, out, sems, out_sem = refs
    slabs, part = len(blocks), blocks[0].shape[0]
    me = lax.axis_index("slab")
    odd = lax.axis_index("subj") % 2 == 1
    copies = []
    for k, block in enumerate(blocks):
        target = fields.at[0, pl.ds((me ^ k) * part, part)]
        copies.append(pltpu.make_async_copy(block, target, sems.at[k]))
        copies[k].start()
    divisor = subjects + MEAN_PRECISION
    for j in range(slabs):
        rows = []
        for i in range(3):
            total = pieces[j, ROWS * i : ROWS * (i + 1)]
            for s in range(1, subjects):
                total = total + pieces[s * slabs + j, ROWS * i : ROWS * (i + 1)]
            rows.append(total / divisor)
        low = low_lanes(rows[0].shape)
        turned = [pltpu.roll(v, CX, 1) for v in rows]
        for i in (0, 1):
            mid = (rows[2], turned[2])
            wide = jnp.where(odd, jnp.where(low, mid[1 - i], turned[i]), rows[i])
            narrow = jnp.where(odd, turned[i], mid[i])
            for n in (0, 1):
                k, here = 4 * j + 2 * i + n, slice(DEPTH * n, DEPTH * (n + 1))
                out[k, :, :LANES] = wide[here] + noise[k, :, :LANES] / math.sqrt(divisor)
                out[k, :, LANES:] = narrow[here, :CX] + noise[k, :, LANES:] / math.sqrt(divisor)
    copies.append(pltpu.make_async_copy(out, new_mean, out_sem))
    copies[-1].start()
    for copy in copies:
        copy.wait()


def finish(pieces, noise, blocks, subjects):
    vmem = pl.BlockSpec(memory_space=pltpu.VMEM)
    anywhere = pl.BlockSpec(memory_space=pl.ANY)
    slabs, (part, depth, cells) = len(blocks), blocks[0].shape
    return pl.pallas_call(
        functools.partial(finish_kernel, subjects=subjects),
        out_shape=[
            jax.ShapeDtypeStruct(noise.shape, jnp.float32),
            jax.ShapeDtypeStruct((1, slabs * part, depth, cells), jnp.float32),
        ],
        in_specs=[vmem] * 2 + [anywhere] * slabs,
        out_specs=[anywhere] * 2,
        scratch_shapes=[
            pltpu.VMEM(noise.shape, jnp.float32),
            pltpu.SemaphoreType.DMA((slabs,)),
            pltpu.SemaphoreType.DMA,
        ],
        compiler_params=pltpu.CompilerParams(vmem_limit_bytes=4 * 2**20),
    )(pieces, noise, *blocks)


def cg_kernel(table, rhs, mean, factor, tissue, *refs, packed, slabs):
    *outs, diag, direction, residual, applied, mean_scratch, total = refs
    blocks, pieces = outs[:-1], outs[-1]
    regressors, depth, cells = rhs.shape
    planes, groups = depth // ROWS, cells // LANES
    everywhere = [(t, g) for t in range(planes) for g in range(groups)]
    low = low_lanes((ROWS, LANES))

    def at(t, g):
        return pl.ds(t * ROWS, ROWS), pl.ds(g * LANES, LANES)

    def tiles_of(ref, r):
        return [[ref[(r,) + at(t, g)] for g in range(groups)] for t in range(planes)]

    def add_up(parts):
        while len(parts) > 1:
            parts = [sum(parts[i : i + 2][1:], parts[i]) for i in range(0, len(parts), 2)]
        return parts[0]

    def reduced(parts):
        own, across, twice = (jnp.sum(p, axis=(0, 1), keepdims=True) for p in parts)
        size = own / across
        return size, size * (twice / across) - 1.0

    def unpack():
        for t, g in everywhere:
            pair, m = g // 3, g % 3
            even, odd = 2 * pair * slabs + 2 * t, (2 * pair + 1) * slabs + 2 * t
            for i in (0, 1):
                two = []
                for j in (0, 1):
                    if m == 1:
                        first, second = mean[even + j, 2 * ROWS :], mean[odd + j, 2 * ROWS :]
                        if i == 0:
                            two.append(jnp.where(low, first, second))
                        else:
                            two.append(pltpu.roll(jnp.where(low, second, first), CX, 1))
                    else:
                        two.append(mean[(even if m == 0 else odd) + j, ROWS * i : ROWS * (i + 1)])
                for n, value in enumerate(mixed(*two)):
                    mean_scratch[(2 * i + n,) + at(t, g)] = value

    def pack_out(t, g, values):
        pair, m = g // 3, g % 3
        even, odd = 2 * pair * slabs + 2 * t, (2 * pair + 1) * slabs + 2 * t
        halves = [mixed(values[2 * i], values[2 * i + 1]) for i in (0, 1)]
        for j in (0, 1):
            first, second = halves[0][j], halves[1][j]
            if m == 1:
                second = pltpu.roll(second, CX, 1)
                pieces[even + j, 2 * ROWS :] = jnp.where(low, first, second)
                pieces[odd + j, 2 * ROWS :] = jnp.where(low, second, first)
            else:
                chunk = (even if m == 0 else odd) + j
                pieces[chunk, :ROWS] = first
                pieces[chunk, ROWS : 2 * ROWS] = second

    def sums(r, tiles, squares, count):
        beside = beside_of(tiles, count)
        across, twice = [], []
        for t, g in everywhere:
            value = diag[(r,) + at(t, g)] * tiles[t][g] - beside[t][g]
            applied[(r,) + at(t, g)] = value
            across.append(tiles[t][g] * value)
            twice.append(value * value)
        return add_up(squares), add_up(across), add_up(twice)

    def begin(r):
        ratio, scale, *kappas = (table[r, i : i + 1] for i in range(2 + CLASSES))
        center = tiles_of(mean_scratch if packed else mean, r)
        beside = beside_of(center, 3)
        squares = []
        for t, g in everywhere:
            where = at(t, g)
            label = tissue[where]
            shifted = 6.0 - inner_neighbours(lax.broadcasted_iota(jnp.int32, label.shape, 1))
            for c in range(CLASSES):
                shifted = shifted + jnp.where(label == c, kappas[c], 0.0)
            diag[(r,) + where] = ratio * factor[where] + shifted
            right = rhs[(r,) + where] + scale * (shifted * center[t][g] - beside[t][g])
            residual[(r,) + where] = right
            direction[(r,) + where] = right
            total[(r,) + where] = jnp.zeros_like(right)
            squares.append(right * right)
            center[t][g] = right
        return sums(r, center, squares, 3)

    def step(r, size, ratio):
        squares, tiles = [], [[None] * groups for _ in range(planes)]
        for t, g in everywhere:
            where = (r,) + at(t, g)
            old = direction[where]
            left = residual[where] - size * applied[where]
            residual[where] = left
            total[where] = total[where] + size * old
            tiles[t][g] = left + ratio * old
            direction[where] = tiles[t][g]
            squares.append(left * left)
        return sums(r, tiles, squares, 2)

    if packed:
        unpack()
    state = tuple(reduced(begin(r)) for r in range(regressors))
    for _ in range(ITERS - 1):
        state = tuple(reduced(step(r, *state[r])) for r in range(regressors))
    for t, g in everywhere:
        values = []
        for r in range(regressors):
            where = (r,) + at(t, g)
            values.append((total[where] + state[r][0] * direction[where]) / table[r, 1:2])
            (total if packed else outs[0])[where] = values[r]
        if packed:
            pack_out(t, g, values)
    if packed:
        me = lax.axis_index("slab")
        for m in range(slabs):

            @pl.when(me == m)
            def _():
                for j in range(slabs):
                    for r in range(regressors):
                        blocks[j ^ m][r] = total[r, DEPTH * j : DEPTH * (j + 1)]


def conjugate_gradients(design, kappa, scale, rhs, mean, factor, tissue, packed, slabs):
    vmem = pl.BlockSpec(memory_space=pltpu.VMEM)
    table = jnp.concatenate([(design / scale)[None], scale[None], kappa])
    table = jnp.pad(table, ((0, ROWS - 2 - CLASSES), (0, 0)))
    table = jnp.broadcast_to(jnp.transpose(table)[:, :, None], (scale.shape[0], ROWS, LANES))
    field = pltpu.VMEM(rhs.shape, jnp.float32)
    part, depth, cells = rhs.shape
    shapes = [(part, depth // slabs, cells)] * slabs + [mean.shape] if packed else [rhs.shape]
    return pl.pallas_call(
        functools.partial(cg_kernel, packed=packed, slabs=slabs),
        out_shape=[jax.ShapeDtypeStruct(s, jnp.float32) for s in shapes],
        in_specs=[vmem] * 5,
        out_specs=[vmem] * len(shapes),
        scratch_shapes=[field] * 6,
        compiler_params=pltpu.CompilerParams(vmem_limit_bytes=32 * 2**20),
    )(table, rhs, mean, factor, tissue)


def nearest_first(blocks, axis):
    me = lax.axis_index(axis)
    return [lax.dynamic_index_in_dim(blocks, me ^ k, 0, keepdims=False) for k in range(lax.axis_size(axis))]


def in_order(near, axis):
    me = lax.axis_index(axis)
    out = jnp.stack(near)
    for k in range(len(near)):
        out = lax.dynamic_update_index_in_dim(out, near[k], me ^ k, 0)
    return out


def swap(block, axis, k):
    return lax.ppermute(block, axis, [(i, i ^ k) for i in range(lax.axis_size(axis))])


def direct(near, axis):
    return [near[0]] + [swap(near[k], axis, k) for k in range(1, len(near))]


def hop(near, axis, bit):
    near = list(near)
    moved = [k for k in range(len(near)) if k & bit]
    got = swap(jnp.stack([near[k] for k in moved]), axis, bit)
    for n, k in enumerate(moved):
        near[k] = got[n]
    return near


def local(
    data_rhs,
    inv_var,
    design,
    keep_mask,
    brain_mask,
    tissue,
    kappa_sq,
    prior_scale,
    mean_field,
    pop_noise,
):
    subjects, slabs = lax.axis_size("subj"), lax.axis_size("slab")
    mine = lax.axis_index("slab")
    total, depth, cells = data_rhs.shape[1:]
    share = mean_field.shape[2]
    part = total // slabs

    packed = fits_packing(part, depth, share, slabs, subjects)
    if packed:
        means = pack(mean_field, subjects, slabs)
    else:
        means = jnp.broadcast_to(mean_field.reshape(1, slabs, part, depth, share), (subjects, slabs, part, depth, share))
        means = means.reshape(subjects * slabs, part, depth, share)
    means = lax.all_to_all(means, ("subj", "slab"), 0, 0, tiled=True)
    if not packed:
        means = means.reshape(subjects, slabs, part, depth, share)
        means = jnp.transpose(means, (2, 1, 3, 0, 4)).reshape(part, slabs * depth, cells)

    bits = [slabs >> n for n in range(1, slabs.bit_length())]
    near = nearest_first(data_rhs.reshape(slabs, part, depth, cells), "slab")
    near = hop(near, "slab", bits[0])
    near, inv_var = lax.optimization_barrier((near, inv_var))
    factor = inv_var * brain_mask.astype(jnp.float32) * keep_mask.astype(jnp.float32)
    planes = jnp.concatenate([factor, tissue.astype(jnp.float32)[None]])
    for bit in bits[1:]:
        near = hop(near, "slab", bit)
    planes = in_order(direct([planes] * slabs, "slab"), "slab")
    blocks = in_order(near, "slab")
    blocks = jnp.transpose(blocks, (1, 0, 2, 3)).reshape(part, slabs * depth, cells)
    planes = jnp.transpose(planes, (1, 0, 2, 3)).reshape(2, slabs * depth, cells)

    fields = conjugate_gradients(
        lax.dynamic_slice_in_dim(design[0], mine * part, part),
        lax.dynamic_slice_in_dim(kappa_sq, mine * part, part, axis=1),
        lax.dynamic_slice_in_dim(prior_scale, mine * part, part),
        blocks,
        means,
        planes[0],
        planes[1].astype(jnp.int32),
        packed,
        slabs,
    )

    if packed:
        *near, pieces = fields
        pieces = lax.all_to_all(pieces, ("subj", "slab"), 0, 0, tiled=True)
        new_mean, solution = finish(pieces, pop_noise, direct(near, "slab"), subjects)
        return solution, new_mean
    by_slab = fields[0].reshape(part, slabs, depth, cells)
    near = nearest_first(jnp.transpose(by_slab, (1, 0, 2, 3)), "slab")
    solution = in_order(direct(near, "slab"), "slab").reshape(1, total, depth, cells)
    pieces = jnp.transpose(by_slab.reshape(part, slabs, depth, subjects, share), (3, 1, 0, 2, 4))
    pieces = pieces.reshape(subjects * slabs, part, depth, share)
    pieces = lax.all_to_all(pieces, ("subj", "slab"), 0, 0, tiled=True)
    summed = jnp.sum(pieces.reshape(subjects, total, depth, share), axis=0)
    divisor = subjects + MEAN_PRECISION
    new_mean = summed / divisor + pop_noise / math.sqrt(divisor)
    return solution, new_mean


def solution(mesh):
    in_specs = (
        P("subj", None, "slab", None),
        P("subj", "slab", None),
        P("subj", None),
        P("subj", "slab", None),
        P("slab", None),
        P("slab", None),
        P(),
        P(),
        P(None, "slab", "subj"),
        P(None, "slab", "subj"),
    )
    out_specs = (P("subj", None, "slab", None), P(None, "slab", "subj"))
    return jax.shard_map(local, mesh=mesh, in_specs=in_specs, out_specs=out_specs, check_vma=False)
```
